512 devices in a mesh: blk: 128 (over y, z, x_lo), rep: 4 (over x_hi, core).
Axes of the slice: x: 4 (x_hi: 2, x_lo: 2; x = x_hi * 2 + x_lo), y: 8, z: 8, core: 2. Of those that a mesh axis runs over, the one named last changes fastest.
Arguments:
- resident_keys: int32 [262144], P('blk'), may hold values from 0 to 4095
- moving_keys: int32 [1048576], P(('blk', 'rep')), may hold values from 0 to 4095
- payload: float32 [1048576, 128], P(('blk', 'rep')), may hold values from -6 to 6
Outputs:
- joined: float32 [262144, 128], P(('blk', 'rep'))
The draws below stay inside these ranges and needn't reach their ends.
All inputs are finite; a program needn't handle non-finite values.
Results may differ from the reference program's by a relative error of at most 0.0003.
Values sent between devices are 32-bit elements; how exact they have to be, the bound alone decides.
No kernel may reach another device: no remote copies, remote signals or barrier semaphores. Data moves between devices by JAX's collectives and lax.ppermute only.
A program may use at most 64 MiB of HBM per device.

```python
import jax
import jax.numpy as jnp
from jax import lax

R_DEV = 2048
S_DEV = 2048
P_SIZE = 128
KEYS = 4096
REACH = 2
R_ROWS = 262144
S_ROWS = 1048576
N_BLK = 128
N_REP = 4


def place_ends(array, stream_key, least, high):
    spot = [jax.random.randint(jax.random.fold_in(stream_key, axis), (), 0, length) for axis, length in enumerate(array.shape)]
    main_axis = array.shape.index(max(array.shape))
    neighbour = spot[:main_axis] + [(spot[main_axis] + 1) % array.shape[main_axis]] + spot[main_axis + 1:]
    return array.at[tuple(spot)].set(least).at[tuple(neighbour)].set(high)


def block_scale(stream_key, shape, pieces, least, high):
    def one(position, shards_of):
        heights = jax.random.uniform(jax.random.fold_in(jax.random.fold_in(stream_key, 6), position), (shards_of,), jnp.float32, least / len(pieces), high / len(pieces))
        return jnp.repeat(jnp.exp(heights), shape[position] // shards_of).reshape((-1,) + (1,) * (len(shape) - position - 1))

    level = one(*pieces[0])
    for cut in pieces[1:]:
        level = level * one(*cut)
    return level


def gaussian(own_key, extent, scale, reach, shards=(), kind=jnp.bfloat16):
    entries = jax.random.normal(own_key, extent, jnp.float32) * scale
    if len(shards) > 0:
        entries = block_scale(own_key, extent, shards, -0.22, 0.18) * entries
    return jnp.clip(entries, min=-reach, max=reach).astype(kind)


def setup_inputs(seed: int = 0) -> dict:
    seeds = jax.random.split(jax.random.key(seed), 4)
    resident_keys = place_ends(jax.random.randint(seeds[0], (R_ROWS,), 0, KEYS), jax.random.fold_in(seeds[0], 1), 0, KEYS - 1).astype(jnp.int32)
    moving_keys = place_ends(jax.random.randint(seeds[1], (S_ROWS,), 0, KEYS), jax.random.fold_in(seeds[1], 1), 0, KEYS - 1).astype(jnp.int32)
    payload = gaussian(seeds[2], (S_ROWS, P_SIZE), 1.0, 6.0, ((0, 512),), jnp.float32)
    return {"resident_keys": resident_keys, "moving_keys": moving_keys, "payload": payload}


def match_block(res_keys, mov_keys, mov_pay):
    hot = (res_keys[:, None] == mov_keys[None, :]).astype(jnp.float32)
    return jnp.dot(hot, mov_pay, precision=lax.Precision.HIGHEST, preferred_element_type=jnp.float32)


def reference(resident_keys, moving_keys, payload):
    res_blocks = resident_keys.reshape(N_BLK, R_DEV)
    key_blocks = moving_keys.reshape(N_BLK, N_REP * S_DEV)
    pay_blocks = payload.reshape(N_BLK, N_REP * S_DEV, P_SIZE)

    def per_block(index):
        res_here = res_blocks[index]
        total = jnp.zeros((R_DEV, P_SIZE), jnp.float32)
        for offset in range(-REACH, REACH + 1):
            source = (index + offset) % N_BLK
            total = total + match_block(res_here, key_blocks[source], pay_blocks[source])
        return total

    joined = lax.map(per_block, jnp.arange(N_BLK, dtype=jnp.int32))
    return joined.reshape(N_BLK * R_DEV, P_SIZE)
```

```python
import functools

import jax
import jax.numpy as jnp
from jax import lax
from jax.experimental import pallas as pl
from jax.experimental.pallas import tpu as pltpu
from jax.sharding import PartitionSpec as P

AXES = ("blk", "rep")
LANES = 128
QUARTER = 512
S_DEV = 2048
KEY_ROWS = 16
MOVING_KEYS = S_DEV // KEY_ROWS
FETCHED_KEYS = MOVING_KEYS + 1
VMEM_LIMIT = 24 * 1024 * 1024
HEAVY = 10**12


def device(block, half, core, blocks):
    return (block % blocks) * 4 + half * 2 + core


def routes(blocks):
    near, far_light, far_heavy, far_heavy_other, fetch, swap, halves = [], [], [], [], [], [], []
    for block in range(blocks):
        low = block % 2
        light = block - 2 if low == 0 else block + 2
        heavy = block + 2 if low == 0 else block - 2
        for half in range(2):
            for core in range(2):
                here = device(block, half, core, blocks)
                x = (half * 2 + low + (1 if core == 0 else -1)) % 4
                near.append((here, device(block - low + x % 2, x // 2, core, blocks)))
                far_light.append((here, device(light, half, core, blocks)))
                far_heavy.append((here, device(heavy, half, core, blocks)))
                far_heavy_other.append((here, device(heavy, 1 - half, core, blocks)))
                fetch.append((device(light if core == 0 else heavy, half, core, blocks), here))
                swap.append((here, device(block, half, 1 - core, blocks)))
                halves.append((here, device(block, 1 - half, core, blocks)))
    return near, far_light, far_heavy, far_heavy_other, fetch, swap, halves


def join_kernel(n_keys, raw, n_add, rows, second_core, n_out, *refs):
    place, refs = refs[0], refs[1:]
    key_refs, refs = refs[:n_keys], refs[n_keys:]
    moving_keys, refs = refs[: len(raw)], refs[len(raw) :]
    moving, refs = refs[: len(raw)], refs[len(raw) :]
    adds, refs = refs[:n_add], refs[n_add:]
    outs, refs = refs[:n_out], refs[n_out:]
    parts, (keys,) = refs[:-1], refs[-1:]
    half, core = place[0], place[1]
    if n_keys == 1:
        keys[...] = key_refs[0][...].astype(jnp.float32)
    else:
        keys[...] = jnp.where(core == second_core, key_refs[0][...], key_refs[1][...])
    columns = []
    for which in rows:
        quarter = (half if which == 0 else 1 - half) * 2 + core
        for j in range(QUARTER // LANES):
            row = keys[pl.ds(quarter * (QUARTER // LANES) + j, 1), :]
            columns.append(jnp.broadcast_to(row, (LANES, LANES)).T)
    resident = jnp.concatenate(columns, axis=0)
    count = resident.shape[0]
    total = jnp.zeros((count, 2 * LANES), jnp.float32)
    parts = list(parts)
    weights = [parts.pop(0) if is_raw else ref for is_raw, ref in zip(raw, moving)]
    for is_raw, ref, split in zip(raw, moving, weights):
        if is_raw:
            value = ref[pl.ds(0, S_DEV), :]
            high = value.astype(jnp.bfloat16)
            split[:, pl.ds(0, LANES)] = high
            split[:, pl.ds(LANES, LANES)] = (value - high.astype(jnp.float32)).astype(jnp.bfloat16)
    for key_rows, split in zip(moving_keys, weights):
        for k in range(S_DEV // 256):
            pieces = []
            for c in range(2):
                mov = key_rows[pl.ds(2 * k + c, 1), :]
                same = resident == jnp.broadcast_to(mov, (count, LANES))
                pieces.append(jnp.where(same, 1.0, 0.0).astype(jnp.bfloat16))
            hot = jnp.concatenate(pieces, axis=1)
            total = total + jnp.dot(hot, split[pl.ds(256 * k, 256), :], preferred_element_type=jnp.float32)
    joined = total[:, :LANES] + total[:, LANES:]
    for extra in adds:
        joined = joined + extra[...]
    each = count // n_out
    for i, out in enumerate(outs):
        out[...] = joined[i * each : (i + 1) * each]


def join(name, place, keys, moving, adds, rows, second_core=0, n_out=1, weight=0):
    count = QUARTER * len(rows)
    whole = pl.BlockSpec(memory_space=pltpu.VMEM)

    def block(height, number):
        return pl.BlockSpec((height, LANES), lambda i: (number, 0))

    raw = tuple(parts is None for _, parts in moving)
    sums = jax.ShapeDtypeStruct((count // n_out, LANES), jnp.float32)
    split = jax.ShapeDtypeStruct((S_DEV, 2 * LANES), jnp.bfloat16)
    return pl.pallas_call(
        functools.partial(join_kernel, len(keys), raw, len(adds), rows, second_core, n_out),
        grid=(1,),
        out_shape=[sums] * n_out + [split] * sum(raw),
        in_specs=[pl.BlockSpec(memory_space=pltpu.SMEM)]
        + [block(KEY_ROWS, number) for _, number in keys]
        + [block(KEY_ROWS, MOVING_KEYS)] * len(moving)
        + [whole] * len(moving)
        + [block(count, number) for _, number in adds],
        out_specs=[whole] * (n_out + sum(raw)),
        scratch_shapes=[pltpu.VMEM((KEY_ROWS, LANES), jnp.float32)],
        compiler_params=pltpu.CompilerParams(vmem_limit_bytes=VMEM_LIMIT),
        cost_estimate=pl.CostEstimate(flops=weight, bytes_accessed=0, transcendentals=0),
        name=name,
    )(
        place,
        *[array for array, _ in keys],
        *[packed for packed, _ in moving],
        *[packed if parts is None else parts for packed, parts in moving],
        *[array for array, _ in adds],
    )


def pack_kernel(payload, keys, packed):
    packed[pl.ds(0, S_DEV), :] = payload[...]
    packed[pl.ds(S_DEV, KEY_ROWS), :] = keys[...].astype(jnp.float32)


def append_kernel(packed, fetched, longer):
    longer[pl.ds(0, S_DEV + KEY_ROWS), :] = packed[...]
    longer[pl.ds(S_DEV + KEY_ROWS, KEY_ROWS), :] = fetched[...].astype(jnp.float32)


def pack(kernel, name, rows, *arrays):
    whole = pl.BlockSpec(memory_space=pltpu.VMEM)
    return pl.pallas_call(
        kernel,
        out_shape=jax.ShapeDtypeStruct((rows, LANES), jnp.float32),
        in_specs=[whole] * len(arrays),
        out_specs=whole,
        compiler_params=pltpu.CompilerParams(vmem_limit_bytes=VMEM_LIMIT),
        name=name,
    )(*arrays)


def local(resident_keys, moving_keys, payload):
    blocks = lax.axis_size("blk")
    near, far_light, far_heavy, far_heavy_other, fetch, swap, halves = routes(blocks)
    send = lambda array, route: lax.ppermute(array, AXES, route)
    rep = lax.axis_index("rep")
    place = jnp.stack([rep // 2, rep % 2]).astype(jnp.int32)
    own_keys = resident_keys.reshape(KEY_ROWS, LANES)
    home_keys = [(own_keys, 0)]

    first = pack(pack_kernel, "pack", S_DEV + KEY_ROWS, payload, moving_keys.reshape(KEY_ROWS, LANES))
    beside = send(first, near)
    fetched = send(own_keys, fetch)
    mine = pack(append_kernel, "append", S_DEV + 2 * KEY_ROWS, first, fetched)
    theirs = send(mine, swap)
    home, mine_parts = join("home_own", place, home_keys, [(mine, None)], [], (0, 1), weight=HEAVY)
    theirs, home, mine_parts = lax.optimization_barrier((theirs, home, mine_parts))

    far_keys = [(mine, FETCHED_KEYS), (theirs, FETCHED_KEYS)]
    light, theirs_parts = join(
        "light", place, far_keys, [(mine, mine_parts), (theirs, None)], [], (0, 1), second_core=0
    )
    light, theirs_parts, beside = lax.optimization_barrier((light, theirs_parts, beside))
    chip = [(mine, mine_parts), (theirs, theirs_parts)]
    light = send(light, far_light)
    beside_theirs = send(beside, swap)
    (heavy,) = join("heavy_own", place, far_keys, chip, [], (0, 1), second_core=1, weight=HEAVY)
    heavy_same, heavy_other, *beside_parts = join(
        "heavy", place, far_keys, [(beside, None), (beside_theirs, None)], [(heavy, 0)], (0, 1), second_core=1, n_out=2
    )
    heavy_other = send(heavy_other, far_heavy_other)
    rest = list(zip([theirs, beside, beside_theirs], [theirs_parts, *beside_parts]))
    (across,) = join("home_other", place, home_keys, rest, [(home, 1), (light, 1)], (1,))
    across = send(across, halves)
    heavy_same = send(heavy_same, far_heavy)
    (kept,) = join("home_same", place, home_keys, rest, [(home, 0), (light, 0), (heavy_other, 0)], (0,))
    return kept + heavy_same + across


def solution(mesh):
    in_specs = (P("blk"), P(("blk", "rep")), P(("blk", "rep"), None))
    out_specs = P(("blk", "rep"), None)
    return jax.shard_map(local, mesh=mesh, in_specs=in_specs, out_specs=out_specs, check_vma=False)
```

```python
import functools

import jax
import jax.numpy as jnp
from jax import lax
from jax.experimental import pallas as pl
from jax.experimental.pallas import tpu as pltpu
from jax.sharding import PartitionSpec as P

AXES = ("blk", "rep")
LANES = 128
QUARTER = 512
S_DEV = 2048
KEY_ROWS = 16
MOVING_KEYS = S_DEV // KEY_ROWS
FETCHED_KEYS = MOVING_KEYS + 1
VMEM_LIMIT = 24 * 1024 * 1024
W_HOME_OWN = 2 * 10**10
W_LIGHT = 0
W_HEAVY_OWN = 0
W_HOME_THEIRS = 2 * 10**10
W_HEAVY = 0
W_HOME_OTHER = 0
W_HOME_SAME = 0


def device(block, half, core, blocks):
    return (block % blocks) * 4 + half * 2 + core


def routes(blocks):
    near, far_light, far_heavy, far_heavy_other, fetch, swap, halves = [], [], [], [], [], [], []
    for block in range(blocks):
        low = block % 2
        light = block - 2 if low == 0 else block + 2
        heavy = block + 2 if low == 0 else block - 2
        for half in range(2):
            for core in range(2):
                here = device(block, half, core, blocks)
                x = (half * 2 + low + (1 if core == 0 else -1)) % 4
                near.append((here, device(block - low + x % 2, x // 2, core, blocks)))
                far_light.append((here, device(light, half, core, blocks)))
                far_heavy.append((here, device(heavy, half, core, blocks)))
                far_heavy_other.append((here, device(heavy, 1 - half, core, blocks)))
                fetch.append((device(light if core == 0 else heavy, half, core, blocks), here))
                swap.append((here, device(block, half, 1 - core, blocks)))
                halves.append((here, device(block, 1 - half, core, blocks)))
    return near, far_light, far_heavy, far_heavy_other, fetch, swap, halves


def join_kernel(n_keys, raw, n_add, rows, second_core, n_out, *refs):
    place, refs = refs[0], refs[1:]
    key_refs, refs = refs[:n_keys], refs[n_keys:]
    moving_keys, refs = refs[: len(raw)], refs[len(raw) :]
    moving, refs = refs[: len(raw)], refs[len(raw) :]
    adds, refs = refs[:n_add], refs[n_add:]
    outs, refs = refs[:n_out], refs[n_out:]
    parts, (keys,) = refs[:-1], refs[-1:]
    half, core = place[0], place[1]
    if n_keys == 1:
        keys[...] = key_refs[0][...].astype(jnp.float32)
    else:
        keys[...] = jnp.where(core == second_core, key_refs[0][...], key_refs[1][...])
    columns = []
    for which in rows:
        quarter = (half if which == 0 else 1 - half) * 2 + core
        for j in range(QUARTER // LANES):
            row = keys[pl.ds(quarter * (QUARTER // LANES) + j, 1), :]
            columns.append(jnp.broadcast_to(row, (LANES, LANES)).T)
    resident = jnp.concatenate(columns, axis=0)
    count = resident.shape[0]
    total = jnp.zeros((count, 2 * LANES), jnp.float32)
    parts = list(parts)
    weights = [parts.pop(0) if is_raw else ref for is_raw, ref in zip(raw, moving)]
    for is_raw, ref, split in zip(raw, moving, weights):
        if is_raw:
            value = ref[pl.ds(0, S_DEV), :]
            high = value.astype(jnp.bfloat16)
            split[:, pl.ds(0, LANES)] = high
            split[:, pl.ds(LANES, LANES)] = (value - high.astype(jnp.float32)).astype(jnp.bfloat16)
    for key_rows, split in zip(moving_keys, weights):
        for k in range(S_DEV // 256):
            pieces = []
            for c in range(2):
                mov = key_rows[pl.ds(2 * k + c, 1), :]
                same = resident == jnp.broadcast_to(mov, (count, LANES))
                pieces.append(jnp.where(same, 1.0, 0.0).astype(jnp.bfloat16))
            hot = jnp.concatenate(pieces, axis=1)
            total = total + jnp.dot(hot, split[pl.ds(256 * k, 256), :], preferred_element_type=jnp.float32)
    joined = total[:, :LANES] + total[:, LANES:]
    for extra in adds:
        joined = joined + extra[...]
    each = count // n_out
    for i, out in enumerate(outs):
        out[...] = joined[i * each : (i + 1) * each]


def join(name, place, keys, moving, adds, rows, second_core=0, n_out=1, weight=0):
    count = QUARTER * len(rows)
    whole = pl.BlockSpec(memory_space=pltpu.VMEM)

    def block(height, number):
        return pl.BlockSpec((height, LANES), lambda i: (number, 0))

    moved = 4 * LANES * (S_DEV * len(moving) + count * (1 + len(adds)))
    raw = tuple(parts is None for _, parts in moving)
    sums = jax.ShapeDtypeStruct((count // n_out, LANES), jnp.float32)
    split = jax.ShapeDtypeStruct((S_DEV, 2 * LANES), jnp.bfloat16)
    return pl.pallas_call(
        functools.partial(join_kernel, len(keys), raw, len(adds), rows, second_core, n_out),
        grid=(1,),
        out_shape=[sums] * n_out + [split] * sum(raw),
        in_specs=[pl.BlockSpec(memory_space=pltpu.SMEM)]
        + [block(KEY_ROWS, number) for _, number in keys]
        + [block(KEY_ROWS, MOVING_KEYS)] * len(moving)
        + [whole] * len(moving)
        + [block(count, number) for _, number in adds],
        out_specs=[whole] * (n_out + sum(raw)),
        scratch_shapes=[pltpu.VMEM((KEY_ROWS, LANES), jnp.float32)],
        compiler_params=pltpu.CompilerParams(vmem_limit_bytes=VMEM_LIMIT),
        cost_estimate=pl.CostEstimate(flops=weight + 4 * count * S_DEV * len(moving) * LANES, bytes_accessed=moved, transcendentals=0),
        name=name,
    )(
        place,
        *[array for array, _ in keys],
        *[packed for packed, _ in moving],
        *[packed if parts is None else parts for packed, parts in moving],
        *[array for array, _ in adds],
    )


def local(resident_keys, moving_keys, payload):
    blocks = lax.axis_size("blk")
    near, far_light, far_heavy, far_heavy_other, fetch, swap, halves = routes(blocks)
    send = lambda array, route: lax.ppermute(array, AXES, route)
    rep = lax.axis_index("rep")
    place = jnp.stack([rep // 2, rep % 2]).astype(jnp.int32)
    own_keys = resident_keys.reshape(KEY_ROWS, LANES)
    home_keys = [(own_keys, 0)]

    def packed(above, keys):
        return jnp.concatenate([above, keys.reshape(KEY_ROWS, LANES).astype(jnp.float32)], axis=0)

    fetched = send(own_keys, fetch)
    first = packed(payload, moving_keys)
    beside = send(first, near)
    mine = packed(first, fetched)
    theirs = send(mine, swap)
    home, mine_parts = join("home_own", place, home_keys, [(first, None)], [], (0, 1), weight=W_HOME_OWN)
    theirs, home, mine_parts = lax.optimization_barrier((theirs, home, mine_parts))

    far_keys = [(mine, FETCHED_KEYS), (theirs, FETCHED_KEYS)]
    light, theirs_parts = join(
        "light", place, far_keys, [(mine, mine_parts), (theirs, None)], [], (0, 1), second_core=0, weight=W_LIGHT
    )
    chip = [(mine, mine_parts), (theirs, theirs_parts)]
    light = send(light, far_light)
    (heavy,) = join("heavy_own", place, far_keys, chip, [], (0, 1), second_core=1, weight=W_HEAVY_OWN)
    beside, heavy = lax.optimization_barrier((beside, heavy))
    beside_theirs = send(beside, swap)
    (home,) = join("home_theirs", place, home_keys, chip[1:], [(home, 0)], (0, 1), weight=W_HOME_THEIRS)
    beside_theirs, home = lax.optimization_barrier((beside_theirs, home))
    heavy_same, heavy_other, *beside_parts = join(
        "heavy", place, far_keys, [(beside, None), (beside_theirs, None)], [(heavy, 0)], (0, 1), second_core=1, n_out=2,
        weight=W_HEAVY,
    )
    heavy_other = send(heavy_other, far_heavy_other)
    rest = list(zip([beside, beside_theirs], beside_parts))
    (across,) = join("home_other", place, home_keys, rest, [(home, 1), (light, 1)], (1,), weight=W_HOME_OTHER)
    across = send(across, halves)
    heavy_same = send(heavy_same, far_heavy)
    (kept,) = join(
        "home_same", place, home_keys, rest, [(home, 0), (light, 0), (heavy_other, 0)], (0,), weight=W_HOME_SAME
    )
    return kept + heavy_same + across


def solution(mesh):
    in_specs = (P("blk"), P(("blk", "rep")), P(("blk", "rep"), None))
    out_specs = P(("blk", "rep"), None)
    return jax.shard_map(local, mesh=mesh, in_specs=in_specs, out_specs=out_specs, check_vma=False)
```

```python
import functools

import jax
import jax.numpy as jnp
from jax import lax
from jax.experimental import pallas as pl
from jax.experimental.pallas import tpu as pltpu
from jax.sharding import PartitionSpec as P

AXES = ("blk", "rep")
LANES = 128
QUARTER = 512
S_DEV = 2048
KEY_ROWS = 16
MOVING_KEYS = S_DEV // KEY_ROWS
FETCHED_KEYS = MOVING_KEYS + 1
VMEM_LIMIT = 24 * 1024 * 1024
W_HOME_OWN = 2 * 10**10
W_LIGHT = 0
W_HEAVY_OWN = 0
W_HOME_THEIRS = 2 * 10**10
W_HEAVY = 0
W_HOME_OTHER = 0
W_HOME_SAME = 0


def device(block, half, core, blocks):
    return (block % blocks) * 4 + half * 2 + core


def routes(blocks):
    near, far_light, far_heavy, far_heavy_other, fetch, swap, halves = [], [], [], [], [], [], []
    for block in range(blocks):
        low = block % 2
        light = block - 2 if low == 0 else block + 2
        heavy = block + 2 if low == 0 else block - 2
        for half in range(2):
            for core in range(2):
                here = device(block, half, core, blocks)
                x = (half * 2 + low + (1 if core == 0 else -1)) % 4
                near.append((here, device(block - low + x % 2, x // 2, core, blocks)))
                far_light.append((here, device(light, half, core, blocks)))
                far_heavy.append((here, device(heavy, half, core, blocks)))
                far_heavy_other.append((here, device(heavy, 1 - half, core, blocks)))
                fetch.append((device(light if core == 0 else heavy, half, core, blocks), here))
                swap.append((here, device(block, half, 1 - core, blocks)))
                halves.append((here, device(block, 1 - half, core, blocks)))
    return near, far_light, far_heavy, far_heavy_other, fetch, swap, halves


def join_kernel(n_in, keys_at, raw, moving_at, parts_at, adds_at, rows, second_core, n_out, *refs):
    ins, outs, splits = refs[:n_in], refs[n_in : n_in + n_out], list(refs[n_in + n_out : -1])
    keys = refs[-1]
    rep = lax.axis_index("rep")
    half, core = rep // 2, rep % 2

    def key_rows(at):
        operand, block = at
        return ins[operand][pl.ds(block * KEY_ROWS, KEY_ROWS), :].astype(jnp.float32)

    if len(keys_at) == 1:
        keys[...] = key_rows(keys_at[0])
    else:
        keys[...] = jnp.where(core == second_core, key_rows(keys_at[0]), key_rows(keys_at[1]))
    columns = []
    for which in rows:
        quarter = (half if which == 0 else 1 - half) * 2 + core
        for j in range(QUARTER // LANES):
            row = keys[pl.ds(quarter * (QUARTER // LANES) + j, 1), :]
            columns.append(jnp.broadcast_to(row, (LANES, LANES)).T)
    resident = jnp.concatenate(columns, axis=0)
    count = resident.shape[0]
    total = jnp.zeros((count, 2 * LANES), jnp.float32)
    weights = [splits.pop(0) if is_raw else ins[at] for is_raw, at in zip(raw, parts_at)]
    for is_raw, at, split in zip(raw, moving_at, weights):
        if is_raw:
            value = ins[at][pl.ds(0, S_DEV), :]
            high = value.astype(jnp.bfloat16)
            split[:, pl.ds(0, LANES)] = high
            split[:, pl.ds(LANES, LANES)] = (value - high.astype(jnp.float32)).astype(jnp.bfloat16)
    for at, split in zip(moving_at, weights):
        for k in range(S_DEV // 256):
            pieces = []
            for c in range(2):
                mov = ins[at][pl.ds(S_DEV + 2 * k + c, 1), :]
                same = resident == jnp.broadcast_to(mov, (count, LANES))
                pieces.append(jnp.where(same, 1.0, 0.0).astype(jnp.bfloat16))
            hot = jnp.concatenate(pieces, axis=1)
            total = total + jnp.dot(hot, split[pl.ds(256 * k, 256), :], preferred_element_type=jnp.float32)
    joined = total[:, :LANES] + total[:, LANES:]
    for at, block in adds_at:
        joined = joined + ins[at][pl.ds(block * count, count), :]
    each = count // n_out
    for i, out in enumerate(outs):
        out[...] = joined[i * each : (i + 1) * each]


def join(name, keys, moving, adds, rows, second_core=0, n_out=1, weight=0):
    count = QUARTER * len(rows)
    whole = pl.BlockSpec(memory_space=pltpu.VMEM)
    operands = []

    def place(array):
        for at, other in enumerate(operands):
            if other is array:
                return at
        operands.append(array)
        return len(operands) - 1

    keys_at = [(place(array), number) for array, number in keys]
    moving_at = [place(packed) for packed, _ in moving]
    parts_at = [None if parts is None else place(parts) for _, parts in moving]
    adds_at = [(place(array), number) for array, number in adds]
    moved = 4 * LANES * (S_DEV * len(moving) + count * (1 + len(adds)))
    raw = tuple(parts is None for _, parts in moving)
    sums = jax.ShapeDtypeStruct((count // n_out, LANES), jnp.float32)
    split = jax.ShapeDtypeStruct((S_DEV, 2 * LANES), jnp.bfloat16)
    return pl.pallas_call(
        functools.partial(
            join_kernel, len(operands), keys_at, raw, moving_at, parts_at, adds_at, rows, second_core, n_out
        ),
        out_shape=[sums] * n_out + [split] * sum(raw),
        in_specs=[whole] * len(operands),
        out_specs=[whole] * (n_out + sum(raw)),
        scratch_shapes=[pltpu.VMEM((KEY_ROWS, LANES), jnp.float32)],
        compiler_params=pltpu.CompilerParams(vmem_limit_bytes=VMEM_LIMIT),
        cost_estimate=pl.CostEstimate(
            flops=weight + 4 * count * S_DEV * len(moving) * LANES, bytes_accessed=moved, transcendentals=0
        ),
        name=name,
    )(*operands)


def local(resident_keys, moving_keys, payload):
    blocks = lax.axis_size("blk")
    near, far_light, far_heavy, far_heavy_other, fetch, swap, halves = routes(blocks)
    send = lambda array, route: lax.ppermute(array, AXES, route)
    own_keys = resident_keys.reshape(KEY_ROWS, LANES)
    home_keys = [(own_keys, 0)]

    def packed(above, keys):
        return jnp.concatenate([above, keys.reshape(KEY_ROWS, LANES).astype(jnp.float32)], axis=0)

    fetched = send(own_keys, fetch)
    first = packed(payload, moving_keys)
    beside = send(first, near)
    mine = packed(first, fetched)
    theirs = send(mine, swap)
    home, mine_parts = join("home_own", home_keys, [(first, None)], [], (0, 1), weight=W_HOME_OWN)
    theirs, home, mine_parts = lax.optimization_barrier((theirs, home, mine_parts))

    far_keys = [(mine, FETCHED_KEYS), (theirs, FETCHED_KEYS)]
    light, theirs_parts = join(
        "light", far_keys, [(mine, mine_parts), (theirs, None)], [], (0, 1), second_core=0, weight=W_LIGHT
    )
    chip = [(mine, mine_parts), (theirs, theirs_parts)]
    light = send(light, far_light)
    (heavy,) = join("heavy_own", far_keys, chip, [], (0, 1), second_core=1, weight=W_HEAVY_OWN)
    beside, heavy = lax.optimization_barrier((beside, heavy))
    beside_theirs = send(beside, swap)
    (home,) = join("home_theirs", home_keys, chip[1:], [(home, 0)], (0, 1), weight=W_HOME_THEIRS)
    beside_theirs, home = lax.optimization_barrier((beside_theirs, home))
    heavy_same, heavy_other, *beside_parts = join(
        "heavy", far_keys, [(beside, None), (beside_theirs, None)], [(heavy, 0)], (0, 1), second_core=1, n_out=2,
        weight=W_HEAVY,
    )
    heavy_other = send(heavy_other, far_heavy_other)
    rest = list(zip([beside, beside_theirs], beside_parts))
    (across,) = join("home_other", home_keys, rest, [(home, 1), (light, 1)], (1,), weight=W_HOME_OTHER)
    across = send(across, halves)
    heavy_same = send(heavy_same, far_heavy)
    (kept,) = join(
        "home_same", home_keys, rest, [(home, 0), (light, 0), (heavy_other, 0)], (0,), weight=W_HOME_SAME
    )
    return kept + heavy_same + across


def solution(mesh):
    in_specs = (P("blk"), P(("blk", "rep")), P(("blk", "rep"), None))
    out_specs = P(("blk", "rep"), None)
    return jax.shard_map(local, mesh=mesh, in_specs=in_specs, out_specs=out_specs, check_vma=False)
```

```python
import functools

import jax
import jax.numpy as jnp
from jax import lax
from jax.experimental import pallas as pl
from jax.experimental.pallas import tpu as pltpu
from jax.sharding import PartitionSpec as P

AXES = ("blk", "rep")
LANES = 128
QUARTER = 512
S_DEV = 2048
KEY_ROWS = 16
MOVING_KEYS = S_DEV // KEY_ROWS
FETCHED_KEYS = MOVING_KEYS + 1
VMEM_LIMIT = 24 * 1024 * 1024
W_HOME_OWN = 2 * 10**10
W_LIGHT = 0
W_HEAVY_OWN = 0
W_HOME_THEIRS = 2 * 10**10
W_HEAVY_BESIDE = 2 * 10**10
W_HEAVY = 0
W_HOME_OTHER = 0
W_HOME_SAME = 0


def device(block, half, core, blocks):
    return (block % blocks) * 4 + half * 2 + core


def routes(blocks):
    near, far_light, far_heavy, far_heavy_other, fetch, swap, halves = [], [], [], [], [], [], []
    for block in range(blocks):
        low = block % 2
        light = block - 2 if low == 0 else block + 2
        heavy = block + 2 if low == 0 else block - 2
        for half in range(2):
            for core in range(2):
                here = device(block, half, core, blocks)
                x = (half * 2 + low + (1 if core == 0 else -1)) % 4
                near.append((here, device(block - low + x % 2, x // 2, core, blocks)))
                far_light.append((here, device(light, half, core, blocks)))
                far_heavy.append((here, device(heavy, half, core, blocks)))
                far_heavy_other.append((here, device(heavy, 1 - half, core, blocks)))
                fetch.append((device(light if core == 0 else heavy, half, core, blocks), here))
                swap.append((here, device(block, half, 1 - core, blocks)))
                halves.append((here, device(block, 1 - half, core, blocks)))
    return near, far_light, far_heavy, far_heavy_other, fetch, swap, halves


def join_kernel(n_in, keys_at, raw, moving_at, parts_at, adds_at, rows, second_core, n_out, *refs):
    ins, outs, splits = refs[:n_in], refs[n_in : n_in + n_out], list(refs[n_in + n_out : -1])
    keys = refs[-1]
    rep = lax.axis_index("rep")
    half, core = rep // 2, rep % 2

    def key_rows(at):
        operand, block = at
        return ins[operand][pl.ds(block * KEY_ROWS, KEY_ROWS), :].astype(jnp.float32)

    if len(keys_at) == 1:
        keys[...] = key_rows(keys_at[0])
    else:
        keys[...] = jnp.where(core == second_core, key_rows(keys_at[0]), key_rows(keys_at[1]))
    columns = []
    for which in rows:
        quarter = (half if which == 0 else 1 - half) * 2 + core
        for j in range(QUARTER // LANES):
            row = keys[pl.ds(quarter * (QUARTER // LANES) + j, 1), :]
            columns.append(jnp.broadcast_to(row, (LANES, LANES)).T)
    resident = jnp.concatenate(columns, axis=0)
    count = resident.shape[0]
    total = jnp.zeros((count, 2 * LANES), jnp.float32)
    weights = [splits.pop(0) if is_raw else ins[at] for is_raw, at in zip(raw, parts_at)]
    for is_raw, at, split in zip(raw, moving_at, weights):
        if is_raw:
            value = ins[at][pl.ds(0, S_DEV), :]
            high = value.astype(jnp.bfloat16)
            split[:, pl.ds(0, LANES)] = high
            split[:, pl.ds(LANES, LANES)] = (value - high.astype(jnp.float32)).astype(jnp.bfloat16)
    for at, split in zip(moving_at, weights):
        for k in range(S_DEV // 256):
            pieces = []
            for c in range(2):
                mov = ins[at][pl.ds(S_DEV + 2 * k + c, 1), :]
                same = resident == jnp.broadcast_to(mov, (count, LANES))
                pieces.append(jnp.where(same, 1.0, 0.0).astype(jnp.bfloat16))
            hot = jnp.concatenate(pieces, axis=1)
            total = total + jnp.dot(hot, split[pl.ds(256 * k, 256), :], preferred_element_type=jnp.float32)
    joined = total[:, :LANES] + total[:, LANES:]
    for at, block in adds_at:
        joined = joined + ins[at][pl.ds(block * count, count), :]
    each = count // n_out
    for i, out in enumerate(outs):
        out[...] = joined[i * each : (i + 1) * each]


def join(name, keys, moving, adds, rows, second_core=0, n_out=1, weight=0):
    count = QUARTER * len(rows)
    whole = pl.BlockSpec(memory_space=pltpu.VMEM)
    operands = []

    def place(array):
        for at, other in enumerate(operands):
            if other is array:
                return at
        operands.append(array)
        return len(operands) - 1

    keys_at = [(place(array), number) for array, number in keys]
    moving_at = [place(packed) for packed, _ in moving]
    parts_at = [None if parts is None else place(parts) for _, parts in moving]
    adds_at = [(place(array), number) for array, number in adds]
    moved = 4 * LANES * (S_DEV * len(moving) + count * (1 + len(adds)))
    raw = tuple(parts is None for _, parts in moving)
    sums = jax.ShapeDtypeStruct((count // n_out, LANES), jnp.float32)
    split = jax.ShapeDtypeStruct((S_DEV, 2 * LANES), jnp.bfloat16)
    return pl.pallas_call(
        functools.partial(
            join_kernel, len(operands), keys_at, raw, moving_at, parts_at, adds_at, rows, second_core, n_out
        ),
        out_shape=[sums] * n_out + [split] * sum(raw),
        in_specs=[whole] * len(operands),
        out_specs=[whole] * (n_out + sum(raw)),
        scratch_shapes=[pltpu.VMEM((KEY_ROWS, LANES), jnp.float32)],
        compiler_params=pltpu.CompilerParams(vmem_limit_bytes=VMEM_LIMIT),
        cost_estimate=pl.CostEstimate(
            flops=weight + 4 * count * S_DEV * len(moving) * LANES, bytes_accessed=moved, transcendentals=0
        ),
        name=name,
    )(*operands)


def local(resident_keys, moving_keys, payload):
    blocks = lax.axis_size("blk")
    near, far_light, far_heavy, far_heavy_other, fetch, swap, halves = routes(blocks)
    send = lambda array, route: lax.ppermute(array, AXES, route)
    own_keys = resident_keys.reshape(KEY_ROWS, LANES)
    home_keys = [(own_keys, 0)]

    def packed(above, keys):
        return jnp.concatenate([above, keys.reshape(KEY_ROWS, LANES).astype(jnp.float32)], axis=0)

    fetched = send(own_keys, fetch)
    first = packed(payload, moving_keys)
    beside = send(first, near)
    mine = packed(first, fetched)
    theirs = send(mine, swap)
    home, mine_parts = join("home_own", home_keys, [(first, None)], [], (0, 1), weight=W_HOME_OWN)
    theirs, home, mine_parts = lax.optimization_barrier((theirs, home, mine_parts))

    far_keys = [(mine, FETCHED_KEYS), (theirs, FETCHED_KEYS)]
    light, theirs_parts = join(
        "light", far_keys, [(mine, mine_parts), (theirs, None)], [], (0, 1), second_core=0, weight=W_LIGHT
    )
    chip = [(mine, mine_parts), (theirs, theirs_parts)]
    light = send(light, far_light)
    (heavy,) = join("heavy_own", far_keys, chip, [], (0, 1), second_core=1, weight=W_HEAVY_OWN)
    (home,) = join("home_theirs", home_keys, chip[1:], [(home, 0)], (0, 1), weight=W_HOME_THEIRS)
    beside, heavy, home = lax.optimization_barrier((beside, heavy, home))
    beside_theirs = send(beside, swap)
    heavy, *beside_parts = join(
        "heavy_beside", far_keys, [(beside, None)], [(heavy, 0)], (0, 1), second_core=1, weight=W_HEAVY_BESIDE
    )
    beside_theirs, heavy = lax.optimization_barrier((beside_theirs, heavy))
    heavy_same, heavy_other, *more_parts = join(
        "heavy", far_keys, [(beside_theirs, None)], [(heavy, 0)], (0, 1), second_core=1, n_out=2, weight=W_HEAVY
    )
    beside_parts = beside_parts + more_parts
    heavy_other = send(heavy_other, far_heavy_other)
    rest = list(zip([beside, beside_theirs], beside_parts))
    (across,) = join("home_other", home_keys, rest, [(home, 1), (light, 1)], (1,), weight=W_HOME_OTHER)
    across = send(across, halves)
    heavy_same = send(heavy_same, far_heavy)
    (kept,) = join(
        "home_same", home_keys, rest, [(home, 0), (light, 0), (heavy_other, 0), (heavy_same, 0)], (0,), weight=W_HOME_SAME
    )
    return kept + across


def solution(mesh):
    in_specs = (P("blk"), P(("blk", "rep")), P(("blk", "rep"), None))
    out_specs = P(("blk", "rep"), None)
    return jax.shard_map(local, mesh=mesh, in_specs=in_specs, out_specs=out_specs, check_vma=False)
```

```python
import functools

import jax
import jax.numpy as jnp
from jax import lax
from jax.experimental import pallas as pl
from jax.experimental.pallas import tpu as pltpu
from jax.sharding import PartitionSpec as P

AXES = ("blk", "rep")
LANES = 128
QUARTER = 512
S_DEV = 2048
KEY_ROWS = 16
MOVING_KEYS = S_DEV // KEY_ROWS
FETCHED_KEYS = MOVING_KEYS + 1
VMEM_LIMIT = 24 * 1024 * 1024
W_HOME_OWN = 2 * 10**10
W_LIGHT = 0
W_HEAVY_OWN = 0
W_HOME_THEIRS = 2 * 10**10
W_HEAVY_BESIDE = 2 * 10**10
W_HEAVY = 0
W_HOME_OTHER = 0
W_HOME_SAME = 0


def device(block, half, core, blocks):
    return (block % blocks) * 4 + half * 2 + core


def routes(blocks):
    near, far_light, far_heavy, far_heavy_other, fetch, swap, halves = [], [], [], [], [], [], []
    for block in range(blocks):
        low = block % 2
        light = block - 2 if low == 0 else block + 2
        heavy = block + 2 if low == 0 else block - 2
        for half in range(2):
            for core in range(2):
                here = device(block, half, core, blocks)
                x = (half * 2 + low + (1 if core == 0 else -1)) % 4
                near.append((here, device(block - low + x % 2, x // 2, core, blocks)))
                far_light.append((here, device(light, half, core, blocks)))
                far_heavy.append((here, device(heavy, half, core, blocks)))
                far_heavy_other.append((here, device(heavy, 1 - half, core, blocks)))
                fetch.append((device(light if core == 0 else heavy, half, core, blocks), here))
                swap.append((here, device(block, half, 1 - core, blocks)))
                halves.append((here, device(block, 1 - half, core, blocks)))
    return near, far_light, far_heavy, far_heavy_other, fetch, swap, halves


def join_kernel(n_in, keys_at, raw, moving_at, parts_at, adds_at, rows, second_core, n_out, *refs):
    ins, outs, splits = refs[:n_in], refs[n_in : n_in + n_out], list(refs[n_in + n_out : -1])
    keys = refs[-1]
    rep = lax.axis_index("rep")
    half, core = rep // 2, rep % 2

    def key_rows(at):
        operand, block = at
        return ins[operand][pl.ds(block * KEY_ROWS, KEY_ROWS), :].astype(jnp.float32)

    if len(keys_at) == 1:
        keys[...] = key_rows(keys_at[0])
    else:
        keys[...] = jnp.where(core == second_core, key_rows(keys_at[0]), key_rows(keys_at[1]))
    columns = []
    for which in rows:
        quarter = (half if which == 0 else 1 - half) * 2 + core
        for j in range(QUARTER // LANES):
            row = keys[pl.ds(quarter * (QUARTER // LANES) + j, 1), :]
            columns.append(jnp.broadcast_to(row, (LANES, LANES)).T)
    resident = jnp.concatenate(columns, axis=0)
    count = resident.shape[0]
    total = jnp.zeros((count, 2 * LANES), jnp.float32)
    weights = [splits.pop(0) if is_raw else ins[at] for is_raw, at in zip(raw, parts_at)]
    for is_raw, at, split in zip(raw, moving_at, weights):
        if is_raw:
            value = ins[at][pl.ds(0, S_DEV), :]
            high = value.astype(jnp.bfloat16)
            split[:, pl.ds(0, LANES)] = high
            split[:, pl.ds(LANES, LANES)] = (value - high.astype(jnp.float32)).astype(jnp.bfloat16)
    for at, split in zip(moving_at, weights):
        for k in range(S_DEV // 256):
            pieces = []
            for c in range(2):
                mov = ins[at][pl.ds(S_DEV + 2 * k + c, 1), :]
                same = resident == jnp.broadcast_to(mov, (count, LANES))
                pieces.append(jnp.where(same, 1.0, 0.0).astype(jnp.bfloat16))
            hot = jnp.concatenate(pieces, axis=1)
            total = total + jnp.dot(hot, split[pl.ds(256 * k, 256), :], preferred_element_type=jnp.float32)
    joined = total[:, :LANES] + total[:, LANES:]
    for at, block in adds_at:
        joined = joined + ins[at][pl.ds(block * count, count), :]
    each = count // n_out
    for i, out in enumerate(outs):
        out[...] = joined[i * each : (i + 1) * each]


def join(name, keys, moving, adds, rows, second_core=0, n_out=1, weight=0):
    count = QUARTER * len(rows)
    whole = pl.BlockSpec(memory_space=pltpu.VMEM)
    operands = []

    def place(array):
        for at, other in enumerate(operands):
            if other is array:
                return at
        operands.append(array)
        return len(operands) - 1

    keys_at = [(place(array), number) for array, number in keys]
    moving_at = [place(packed) for packed, _ in moving]
    parts_at = [None if parts is None else place(parts) for _, parts in moving]
    adds_at = [(place(array), number) for array, number in adds]
    moved = 4 * LANES * (S_DEV * len(moving) + count * (1 + len(adds)))
    raw = tuple(parts is None for _, parts in moving)
    sums = jax.ShapeDtypeStruct((count // n_out, LANES), jnp.float32)
    split = jax.ShapeDtypeStruct((S_DEV, 2 * LANES), jnp.bfloat16)
    return pl.pallas_call(
        functools.partial(
            join_kernel, len(operands), keys_at, raw, moving_at, parts_at, adds_at, rows, second_core, n_out
        ),
        out_shape=[sums] * n_out + [split] * sum(raw),
        in_specs=[whole] * len(operands),
        out_specs=[whole] * (n_out + sum(raw)),
        scratch_shapes=[pltpu.VMEM((KEY_ROWS, LANES), jnp.float32)],
        compiler_params=pltpu.CompilerParams(vmem_limit_bytes=VMEM_LIMIT),
        cost_estimate=pl.CostEstimate(
            flops=weight + 4 * count * S_DEV * len(moving) * LANES, bytes_accessed=moved, transcendentals=0
        ),
        name=name,
    )(*operands)


def local(resident_keys, moving_keys, payload):
    blocks = lax.axis_size("blk")
    near, far_light, far_heavy, far_heavy_other, fetch, swap, halves = routes(blocks)
    send = lambda array, route: lax.ppermute(array, AXES, route)
    own_keys = resident_keys.reshape(KEY_ROWS, LANES)
    home_keys = [(own_keys, 0)]

    def packed(above, keys):
        return jnp.concatenate([above, keys.reshape(KEY_ROWS, LANES).astype(jnp.float32)], axis=0)

    fetched = send(own_keys, fetch)
    key_rows = jnp.pad(moving_keys.reshape(KEY_ROWS, LANES), ((S_DEV, 0), (0, 0))).astype(jnp.float32)
    first = jnp.pad(payload, ((0, KEY_ROWS), (0, 0))) + key_rows
    beside = send(first, near)
    mine = packed(first, fetched)
    theirs = send(mine, swap)
    home, mine_parts = join("home_own", home_keys, [(first, None)], [], (0, 1), weight=W_HOME_OWN)
    theirs, home, mine_parts = lax.optimization_barrier((theirs, home, mine_parts))

    far_keys = [(mine, FETCHED_KEYS), (theirs, FETCHED_KEYS)]
    light, theirs_parts = join(
        "light", far_keys, [(mine, mine_parts), (theirs, None)], [], (0, 1), second_core=0, weight=W_LIGHT
    )
    chip = [(mine, mine_parts), (theirs, theirs_parts)]
    light = send(light, far_light)
    (heavy,) = join("heavy_own", far_keys, chip, [], (0, 1), second_core=1, weight=W_HEAVY_OWN)
    (home,) = join("home_theirs", home_keys, chip[1:], [(home, 0)], (0, 1), weight=W_HOME_THEIRS)
    beside, heavy, home = lax.optimization_barrier((beside, heavy, home))
    beside_theirs = send(beside, swap)
    heavy, *beside_parts = join(
        "heavy_beside", far_keys, [(beside, None)], [(heavy, 0)], (0, 1), second_core=1, weight=W_HEAVY_BESIDE
    )
    beside_theirs, heavy = lax.optimization_barrier((beside_theirs, heavy))
    heavy_same, heavy_other, *more_parts = join(
        "heavy", far_keys, [(beside_theirs, None)], [(heavy, 0)], (0, 1), second_core=1, n_out=2, weight=W_HEAVY
    )
    beside_parts = beside_parts + more_parts
    heavy_other = send(heavy_other, far_heavy_other)
    rest = list(zip([beside, beside_theirs], beside_parts))
    (across,) = join("home_other", home_keys, rest, [(home, 1), (light, 1)], (1,), weight=W_HOME_OTHER)
    across = send(across, halves)
    heavy_same = send(heavy_same, far_heavy)
    (kept,) = join(
        "home_same", home_keys, rest, [(home, 0), (light, 0), (heavy_other, 0), (heavy_same, 0)], (0,), weight=W_HOME_SAME
    )
    return kept + across


def solution(mesh):
    in_specs = (P("blk"), P(("blk", "rep")), P(("blk", "rep"), None))
    out_specs = P(("blk", "rep"), None)
    return jax.shard_map(local, mesh=mesh, in_specs=in_specs, out_specs=out_specs, check_vma=False)
```

```python
import functools

import jax
import jax.numpy as jnp
from jax import lax
from jax.experimental import pallas as pl
from jax.experimental.pallas import tpu as pltpu
from jax.sharding import PartitionSpec as P

AXES = ("blk", "rep")
LANES = 128
QUARTER = 512
S_DEV = 2048
KEY_ROWS = 16
MOVING_KEYS = S_DEV // KEY_ROWS
FETCHED_KEYS = MOVING_KEYS + 1
VMEM_LIMIT = 24 * 1024 * 1024
W_HOME_OWN = 2 * 10**10
W_LIGHT = 0
W_HEAVY_OWN = 0
W_HOME_THEIRS = 2 * 10**10
W_HEAVY_BESIDE = 2 * 10**10
W_HEAVY = 0
W_HOME_OTHER = 0
W_HOME_SAME = 0


def device(block, half, core, blocks):
    return (block % blocks) * 4 + half * 2 + core


def routes(blocks):
    near, far_light, far_heavy, far_heavy_other, fetch, swap, halves = [], [], [], [], [], [], []
    for block in range(blocks):
        low = block % 2
        light = block - 2 if low == 0 else block + 2
        heavy = block + 2 if low == 0 else block - 2
        for half in range(2):
            for core in range(2):
                here = device(block, half, core, blocks)
                x = (half * 2 + low + (1 if core == 0 else -1)) % 4
                near.append((here, device(block - low + x % 2, x // 2, core, blocks)))
                far_light.append((here, device(light, half, core, blocks)))
                far_heavy.append((here, device(heavy, half, core, blocks)))
                far_heavy_other.append((here, device(heavy, 1 - half, core, blocks)))
                fetch.append((device(light if core == 0 else heavy, half, core, blocks), here))
                swap.append((here, device(block, half, 1 - core, blocks)))
                halves.append((here, device(block, 1 - half, core, blocks)))
    return near, far_light, far_heavy, far_heavy_other, fetch, swap, halves


def join_kernel(n_in, keys_at, raw, moving_at, parts_at, adds_at, rows, second_core, n_out, *refs):
    ins, outs, splits = refs[:n_in], refs[n_in : n_in + n_out], list(refs[n_in + n_out : -1])
    keys = refs[-1]
    rep = lax.axis_index("rep")
    half, core = rep // 2, rep % 2

    def key_rows(at):
        operand, block = at
        return ins[operand][pl.ds(block * KEY_ROWS, KEY_ROWS), :].astype(jnp.float32)

    if len(keys_at) == 1:
        keys[...] = key_rows(keys_at[0])
    else:
        keys[...] = jnp.where(core == second_core, key_rows(keys_at[0]), key_rows(keys_at[1]))
    columns = []
    for which in rows:
        quarter = (half if which == 0 else 1 - half) * 2 + core
        for j in range(QUARTER // LANES):
            row = keys[pl.ds(quarter * (QUARTER // LANES) + j, 1), :]
            columns.append(jnp.broadcast_to(row, (LANES, LANES)).T)
    resident = jnp.concatenate(columns, axis=0)
    count = resident.shape[0]
    total = jnp.zeros((count, 2 * LANES), jnp.float32)
    weights = [splits.pop(0) if is_raw else ins[at] for is_raw, at in zip(raw, parts_at)]
    for is_raw, at, split in zip(raw, moving_at, weights):
        if is_raw:
            value = ins[at][pl.ds(0, S_DEV), :]
            high = value.astype(jnp.bfloat16)
            split[:, pl.ds(0, LANES)] = high
            split[:, pl.ds(LANES, LANES)] = (value - high.astype(jnp.float32)).astype(jnp.bfloat16)
    for at, split in zip(moving_at, weights):
        for k in range(S_DEV // 256):
            pieces = []
            for c in range(2):
                mov = ins[at][pl.ds(S_DEV + 2 * k + c, 1), :]
                same = resident == jnp.broadcast_to(mov, (count, LANES))
                pieces.append(jnp.where(same, 1.0, 0.0).astype(jnp.bfloat16))
            hot = jnp.concatenate(pieces, axis=1)
            total = total + jnp.dot(hot, split[pl.ds(256 * k, 256), :], preferred_element_type=jnp.float32)
    joined = total[:, :LANES] + total[:, LANES:]
    for at, block in adds_at:
        joined = joined + ins[at][pl.ds(block * count, count), :]
    each = count // n_out
    for i, out in enumerate(outs):
        out[...] = joined[i * each : (i + 1) * each]


def join(name, keys, moving, adds, rows, second_core=0, n_out=1, weight=0):
    count = QUARTER * len(rows)
    whole = pl.BlockSpec(memory_space=pltpu.VMEM)
    operands = []

    def place(array):
        for at, other in enumerate(operands):
            if other is array:
                return at
        operands.append(array)
        return len(operands) - 1

    keys_at = [(place(array), number) for array, number in keys]
    moving_at = [place(packed) for packed, _ in moving]
    parts_at = [None if parts is None else place(parts) for _, parts in moving]
    adds_at = [(place(array), number) for array, number in adds]
    moved = 4 * LANES * (S_DEV * len(moving) + count * (1 + len(adds)))
    raw = tuple(parts is None for _, parts in moving)
    sums = jax.ShapeDtypeStruct((count // n_out, LANES), jnp.float32)
    split = jax.ShapeDtypeStruct((S_DEV, 2 * LANES), jnp.bfloat16)
    return pl.pallas_call(
        functools.partial(
            join_kernel, len(operands), keys_at, raw, moving_at, parts_at, adds_at, rows, second_core, n_out
        ),
        out_shape=[sums] * n_out + [split] * sum(raw),
        in_specs=[whole] * len(operands),
        out_specs=[whole] * (n_out + sum(raw)),
        scratch_shapes=[pltpu.VMEM((KEY_ROWS, LANES), jnp.float32)],
        compiler_params=pltpu.CompilerParams(vmem_limit_bytes=VMEM_LIMIT),
        cost_estimate=pl.CostEstimate(
            flops=weight + 4 * count * S_DEV * len(moving) * LANES, bytes_accessed=moved, transcendentals=0
        ),
        name=name,
    )(*operands)


def local(resident_keys, moving_keys, payload):
    blocks = lax.axis_size("blk")
    near, far_light, far_heavy, far_heavy_other, fetch, swap, halves = routes(blocks)
    send = lambda array, route: lax.ppermute(array, AXES, route)
    own_keys = resident_keys.reshape(KEY_ROWS, LANES)
    home_keys = [(own_keys, 0)]

    fetched = send(own_keys, fetch)
    key_rows = jnp.pad(moving_keys.reshape(KEY_ROWS, LANES), ((S_DEV, 0), (0, 0))).astype(jnp.float32)
    first = jnp.pad(payload, ((0, KEY_ROWS), (0, 0))) + key_rows
    beside = send(first, near)
    fetched_rows = jnp.pad(fetched, ((S_DEV + KEY_ROWS, 0), (0, 0))).astype(jnp.float32)
    mine = jnp.pad(first, ((0, KEY_ROWS), (0, 0))) + fetched_rows
    theirs = send(mine, swap)
    home, mine_parts = join("home_own", home_keys, [(first, None)], [], (0, 1), weight=W_HOME_OWN)
    theirs, home, mine_parts = lax.optimization_barrier((theirs, home, mine_parts))

    far_keys = [(mine, FETCHED_KEYS), (theirs, FETCHED_KEYS)]
    light, theirs_parts = join(
        "light", far_keys, [(mine, mine_parts), (theirs, None)], [], (0, 1), second_core=0, weight=W_LIGHT
    )
    chip = [(mine, mine_parts), (theirs, theirs_parts)]
    light = send(light, far_light)
    (heavy,) = join("heavy_own", far_keys, chip, [], (0, 1), second_core=1, weight=W_HEAVY_OWN)
    (home,) = join("home_theirs", home_keys, chip[1:], [(home, 0)], (0, 1), weight=W_HOME_THEIRS)
    beside, heavy, home = lax.optimization_barrier((beside, heavy, home))
    beside_theirs = send(beside, swap)
    heavy, *beside_parts = join(
        "heavy_beside", far_keys, [(beside, None)], [(heavy, 0)], (0, 1), second_core=1, weight=W_HEAVY_BESIDE
    )
    beside_theirs, heavy = lax.optimization_barrier((beside_theirs, heavy))
    heavy_same, heavy_other, *more_parts = join(
        "heavy", far_keys, [(beside_theirs, None)], [(heavy, 0)], (0, 1), second_core=1, n_out=2, weight=W_HEAVY
    )
    beside_parts = beside_parts + more_parts
    heavy_other = send(heavy_other, far_heavy_other)
    rest = list(zip([beside, beside_theirs], beside_parts))
    (across,) = join("home_other", home_keys, rest, [(home, 1), (light, 1)], (1,), weight=W_HOME_OTHER)
    across = send(across, halves)
    heavy_same = send(heavy_same, far_heavy)
    (kept,) = join(
        "home_same", home_keys, rest, [(home, 0), (light, 0), (heavy_other, 0), (heavy_same, 0)], (0,), weight=W_HOME_SAME
    )
    return kept + across


def solution(mesh):
    in_specs = (P("blk"), P(("blk", "rep")), P(("blk", "rep"), None))
    out_specs = P(("blk", "rep"), None)
    return jax.shard_map(local, mesh=mesh, in_specs=in_specs, out_specs=out_specs, check_vma=False)
```
